32 devices in a mesh: ctx: 8 (over z, y), head: 4 (over x, core).
Axes of the slice: x: 2, y: 2, z: 4, core: 2. Of those that a mesh axis runs over, the one named last changes fastest.
Arguments:
- queries: bfloat16 [2048, 2048], P('ctx', 'head'), may hold values from -6 to 6
- key_rows: bfloat16 [2048, 2048], P('ctx', 'head'), may hold values from -1.5 to 1.5
- value_rows: bfloat16 [2048, 2048], P('ctx', 'head'), may hold values from -6 to 6
- carry_state: float32 [16, 128, 128], P('head'), may hold values from -96 to 96
- decay_rate: float32 [16], P('head'), as said below
- norm_gain: float32 [2048], P('head'), may hold values from 0.5 to 1.5
- order: int32 [8, 256], P('ctx'), may hold values from 0 to 255, each once within a row
- doc_lengths: int32 [16], replicated, may hold values from 1 to 1024, 2048 in all
Outputs:
- mixed: bfloat16 [2048, 2048], P('ctx', 'head')
The draws below stay inside these ranges and needn't reach their ends.
Inputs may be any that keep to these rules, and one draw needn't show every extreme that they name: `order`: each row is a permutation of 0..255. `doc_lengths`: they sum to 2048; the longest is exactly 1024. `decay_rate`: positive rates.
All inputs are finite; a program needn't handle non-finite values.
Results may differ from the reference program's by a relative error of at most 0.001.
Values may be sent and summed in bfloat16 or wider, within the bound.
A program may use at most 128 MiB of HBM per device.

```python
import math
import jax
import jax.numpy as jnp
import numpy as np
from jax import lax

TOK_DEV = 256
DH = 128
HEADS = 16
TOKENS = 2048
SPILL = 64
BLOCK = 256
DOC_MOST = 1024
NDOCS = 16
N_CTX = 8


def draw_decay_rate(key, part):
    pick_key, fast_key, slow_key = jax.random.split(jax.random.fold_in(key, 7), 3)
    fast_share = 0.5
    is_fast = jax.random.uniform(pick_key, (HEADS,), jnp.float32) < fast_share
    fast_rate = jnp.exp(jax.random.uniform(fast_key, (HEADS,), jnp.float32, jnp.log(1.0 / 50.0), jnp.log(1.0 / 30.0)))
    slow_rate = jnp.exp(jax.random.uniform(slow_key, (HEADS,), jnp.float32, jnp.log(0.05), jnp.log(2.0))) / DOC_MOST
    return jnp.where(is_fast, fast_rate, slow_rate).astype(jnp.float32)


def steps_of(rng, extent, cuts, smallest, high):
    loudness = 1.0
    for dim, blocks in cuts:
        heights = jax.random.uniform(jax.random.fold_in(jax.random.fold_in(rng, 6), dim), (blocks,), jnp.float32, smallest / len(cuts), high / len(cuts))
        loudness = loudness * jnp.repeat(jnp.exp(heights), extent[dim] // blocks).reshape((-1,) + (1,) * (len(extent) - 1 - dim))
    return loudness


def length_profile(amount, total, most, lean):
    portions = [(1 << 20) // math.isqrt(standing ** lean) + 1 for standing in range(2, amount + 1)]
    surplus, given = total - most - (amount - 1), [1] * (amount - 1)
    while surplus > 0:
        movable = [i for i in range(amount - 1) if given[i] < most]
        pool, remaining = sum([portions[i] for i in movable]), surplus
        for i in movable:
            extra = min(most - given[i], max(1, remaining * portions[i] // pool), surplus)
            given[i] = given[i] + extra
            surplus = surplus - extra
    return np.array([most] + given)


def ragged(stream_key, count, total, bound, skew):
    if count == 2:
        one = jax.random.randint(stream_key, (), max(1, total - bound), min(bound, total - 1) + 1)
        return jnp.stack([one, total - one])
    sizes = jnp.asarray(length_profile(count, total, bound, skew), jnp.int32)
    couples = (count - 1) // 2
    donor, receiver = sizes[1:1 + 2 * couples:2], sizes[2:2 + 2 * couples:2]
    slack = jnp.minimum(donor - 1, bound - receiver)
    shifted = jax.random.randint(jax.random.fold_in(stream_key, 1), (couples,), 0, 1 << 20) % (slack + 1)
    sizes = sizes.at[1:1 + 2 * couples:2].set(donor - shifted).at[2:2 + 2 * couples:2].set(receiver + shifted)
    return sizes[jax.random.permutation(jax.random.fold_in(stream_key, 2), count)]


def centred(key, extent, scale, bound, cuts=(), held_as=jnp.bfloat16):
    level = steps_of(key, extent, cuts, -0.22, 0.18) if cuts else 1.0
    array = jax.random.normal(key, extent, jnp.float32) * scale * level
    return jnp.minimum(jnp.maximum(array, -bound), bound).astype(held_as)


def setup_inputs(seed: int = 0) -> dict:
    arg_keys = jax.random.split(jax.random.key(seed), 9)
    return {
        "queries": centred(arg_keys[0], (TOKENS, HEADS * DH), 1.0, 6.0, ((0, 8), (1, 4))),
        "key_rows": centred(arg_keys[1], (TOKENS, HEADS * DH), 0.25, 1.5, ((0, 8), (1, 4))),
        "value_rows": centred(arg_keys[2], (TOKENS, HEADS * DH), 1.0, 6.0, ((0, 8), (1, 4))),
        "carry_state": centred(arg_keys[3], (HEADS, DH, DH), 16.0, 96.0, ((0, 4),), jnp.float32),
        "decay_rate": draw_decay_rate(jax.random.fold_in(arg_keys[8], 71), 0),
        "norm_gain": jnp.clip(1.0 + 0.1 * jax.random.normal(arg_keys[5], (HEADS * DH,), jnp.float32), 0.5, 1.5),
        "order": jax.vmap(lambda own: jax.random.permutation(own, TOK_DEV))(jax.random.split(arg_keys[6], N_CTX)).reshape((N_CTX, TOK_DEV)).astype(jnp.int32),
        "doc_lengths": ragged(arg_keys[7], NDOCS, TOKENS, DOC_MOST, 2).astype(jnp.int32),
    }


def reference(queries, key_rows, value_rows, carry_state, decay_rate, norm_gain, order, doc_lengths):
    devices = jnp.arange(N_CTX, dtype=jnp.int32)[:, None]
    columns = jnp.arange(TOK_DEV, dtype=jnp.int32)[None, :]
    following = (devices + 1) % N_CTX
    source = jnp.where(columns < TOK_DEV - SPILL, devices * TOK_DEV + order, following * TOK_DEV + order[following[:, 0]])
    source = source.reshape(-1).astype(jnp.int32)
    doc_ends = jnp.cumsum(doc_lengths).astype(jnp.int32)
    positions = jnp.arange(TOKENS, dtype=jnp.int32)
    segment = jnp.searchsorted(doc_ends, positions, side='right').astype(jnp.int32)
    block_count = TOKENS // BLOCK
    starts = jnp.arange(block_count, dtype=jnp.int32) * BLOCK - 1
    previous = jnp.searchsorted(doc_ends, starts, side='right').astype(jnp.int32)
    shape = (block_count, BLOCK, HEADS, DH)
    ctx_query = queries[source].reshape(shape)
    ctx_key = key_rows[source].reshape(shape)
    ctx_value = value_rows[source].reshape(shape)
    segments = segment.reshape(block_count, BLOCK)
    rates = decay_rate.astype(jnp.float32)
    offsets = jnp.arange(BLOCK, dtype=jnp.int32)
    distance = offsets[:, None] - offsets[None, :]
    lower = distance >= 0
    decay = jnp.exp(-rates[:, None, None] * jnp.maximum(distance, 0).astype(jnp.float32)[None])
    leading = jnp.exp(-rates[None, :] * (offsets + 1).astype(jnp.float32)[:, None])
    trailing = jnp.exp(-rates[None, :] * (BLOCK - 1 - offsets).astype(jnp.float32)[:, None])
    whole_block = jnp.exp(-rates * jnp.float32(BLOCK))
    highest = lax.Precision.HIGHEST
    gains = norm_gain.astype(jnp.float32)

    def block_step(running, inputs):
        query_f, key_f, value_f, seg_ids, prior = inputs
        query_f = query_f.astype(jnp.float32)
        key_f = key_f.astype(jnp.float32)
        value_f = value_f.astype(jnp.float32)
        same_doc = (seg_ids[:, None] == seg_ids[None, :]) & lower
        scores = jnp.einsum('thd,shd->hts', query_f, key_f, precision=highest)
        weights = jnp.where(same_doc[None], scores * decay, jnp.float32(0.0))
        attn = jnp.einsum('hts,shd->thd', weights, value_f, precision=highest)
        carry_on = (seg_ids == prior).astype(jnp.float32)
        inter = jnp.einsum('thd,hde->the', query_f, running, precision=highest)
        attn = attn + inter * (leading * carry_on[:, None])[:, :, None]
        at_end = (seg_ids == seg_ids[-1]).astype(jnp.float32)
        added = jnp.einsum('shd,she->hde', key_f * (trailing * at_end[:, None])[:, :, None], value_f, precision=highest)
        keep_factor = jnp.where(seg_ids[-1] == prior, whole_block, jnp.float32(0.0))
        running = keep_factor[:, None, None] * running + added
        flat = attn.reshape(BLOCK, HEADS * DH)
        mean_sq = lax.optimization_barrier(jnp.mean(flat * flat, axis=1, keepdims=True))
        normed = (flat * lax.rsqrt(mean_sq + 1e-05) * gains[None, :]).astype(jnp.bfloat16)
        return (running, normed)
    _, outputs = lax.scan(block_step, carry_state.astype(jnp.float32), (ctx_query, ctx_key, ctx_value, segments, previous))
    result = jnp.zeros((TOKENS, HEADS * DH), jnp.bfloat16)
    return result.at[source].set(outputs.reshape(TOKENS, HEADS * DH))
```

```python
import functools

import jax
import jax.numpy as jnp
from jax import lax
from jax.experimental import pallas as pl
from jax.experimental.pallas import tpu as pltpu
from jax.sharding import PartitionSpec as P

F32 = jnp.float32
BF16 = jnp.bfloat16
MESH = pl.DeviceIdType.MESH


def split(x):
    high = x.astype(BF16)
    return high, (x - high.astype(F32)).astype(BF16)


def dot(a, b, contract):
    return lax.dot_general(a, b, ((contract[:1], contract[1:]), ((), ())), preferred_element_type=F32)


def two_term(a, b, contract):
    width = b.shape[1]
    both = dot(a, jnp.concatenate(split(b), axis=1), contract)
    return both[:, :width] + both[:, width:]


def kernel(
    n_ctx, n_head, reach,
    rate_ref, docs_ref, q_ref, k_ref, v_ref, carry_ref, gain_ref, order_ref, out_ref,
    attn, pair, away, layer, landed, onward, arrived, squares, squares_in,
    pair_send, pair_recv, layer_send, layer_recv, onward_send, onward_recv, sq_send, sq_recv,
):
    rows, features = q_ref.shape
    heads = rate_ref.shape[0]
    width = features // heads
    half = heads // 2
    n_docs = docs_ref.shape[0]
    spill = rows // 4
    keep = rows - spill
    tokens = n_ctx * rows
    n_pairs = n_ctx // 2
    d = lax.axis_index("ctx")
    g = lax.axis_index("head")
    u = d // 2
    y = lax.rem(d, 2)
    partner = d + 1 - 2 * y
    mine = y * half
    other = (1 - y) * half

    def sends(b):
        return u + b <= n_pairs

    def receives(b):
        return (u >= b) | (u == 0)

    barrier = pltpu.get_barrier_semaphore()
    pl.semaphore_signal(barrier, inc=1, device_id=(partner, g), device_id_type=MESH)
    for j in range(1, n_head):
        pl.semaphore_signal(
            barrier, inc=1, device_id=(d, lax.rem(g + n_head - j, n_head)), device_id_type=MESH
        )
    expected = jnp.int32(n_head)
    for b in range(1, reach + 1):
        @pl.when(receives(b))
        def _():
            source = lax.rem(u + n_pairs - b, n_pairs) * 2 + y
            pl.semaphore_signal(barrier, inc=1, device_id=(source, g), device_id_type=MESH)
        expected = expected + sends(b).astype(jnp.int32)

    base = jnp.where(d == 0, tokens, d * rows) - spill
    last = d * rows + keep - 1
    chosen = (order_ref[...] == lax.broadcasted_iota(jnp.int32, (rows, rows), 0)).astype(F32).astype(BF16)
    index = lax.broadcasted_iota(jnp.int32, (rows, rows), 0).astype(F32).astype(BF16)
    along = lax.broadcasted_iota(jnp.int32, (16, rows), 1).astype(F32).astype(BF16)

    def position(slot):
        kept_at = (d * rows).astype(F32)
        moved_at = (base - keep).astype(F32)
        return slot + jnp.where(slot < keep, kept_at, moved_at)

    down = position(dot(chosen, index, (1, 0)))
    across = position(dot(along, chosen, (1, 1)))[0:1]
    pos = down[:, :width]

    pair_last = 2 * u * rows + rows + keep - 1
    first_last = 2 * u * rows + keep - 1
    pair_base = jnp.where(u == 0, tokens, 2 * u * rows) - spill
    marks = (last, pair_last, first_last, pair_base - 1)

    def document(n, carried):
        edge, begin, scalars = carried
        edge = edge + docs_ref[n]
        mark = edge.astype(F32)
        begin = jnp.where(pos >= mark, mark, begin)
        return edge, begin, tuple(jnp.where(m >= edge, edge, s) for m, s in zip(marks, scalars))

    zero = jnp.int32(0)
    state = (zero, jnp.zeros((rows, width), F32), (zero,) * 4)
    if n_docs <= 32:
        for n in range(n_docs):
            state = document(n, state)
    else:
        state = lax.fori_loop(0, n_docs, document, state)
    _, begin, (last_begin, pair_begin, first_begin, base_begin) = state

    inf = jnp.float32(jnp.inf)

    def decay(h, steps):
        return jnp.exp(-rate_ref[h] * steps)

    def factor(h, steps, holds):
        return decay(h, jnp.full((1, width), jnp.where(holds, jnp.float32(steps), inf)))

    def columns(ref, h):
        return ref[:, pl.ds(pl.multiple_of(h * width, width), width)]

    to_last = jnp.where((pos <= last.astype(F32)) & (pos >= last_begin.astype(F32)), last.astype(F32) - pos, inf)

    def own_state(h):
        weighted = columns(v_ref, h).astype(F32) * decay(h, to_last)
        return two_term(columns(k_ref, h), weighted, (0, 0))

    def copy(src, dst, send, recv, target):
        return pltpu.make_async_remote_copy(
            src_ref=src, dst_ref=dst, send_sem=send, recv_sem=recv, device_id=target, device_id_type=MESH
        )

    pair_copies = []
    for i in range(half):
        away[i] = own_state(other + i)
        if i == 0:
            pl.semaphore_wait(barrier, expected)
        c = copy(away.at[i], pair.at[y, i], pair_send.at[i], pair_recv.at[i], (partner, g))
        c.start()
        pair_copies.append(c)
    for i in range(half):
        pair[y, i] = own_state(mine + i)

    def layer_copy(b, i):
        target = lax.rem(u + b, n_pairs) * 2 + y
        return copy(layer.at[i], landed.at[b - 1, i], layer_send.at[b - 1, i], layer_recv.at[b - 1, i], (target, g))

    for i in range(half):
        pair_copies[i].wait_recv()
        layer[i] = pair[1, i] + factor(mine + i, rows, pair_begin <= pair_last - rows) * pair[0, i]
        for b in range(1, reach + 1):
            @pl.when(sends(b))
            def _():
                layer_copy(b, i).start()

    gap = down - across
    begins = jnp.concatenate([begin] * (rows // width), axis=1)
    gap = jnp.where((gap >= 0) & (across >= begins), gap, inf)
    to_carry = jnp.where(begin == 0, pos + 1, inf)
    for h in range(heads):
        cols = slice(h * width, (h + 1) * width)
        q, v = q_ref[:, cols], v_ref[:, cols]
        weights = dot(q, k_ref[:, cols], (1, 1)) * decay(h, gap)
        high, low = split(weights)
        local = dot(high, v, (1, 0)) + dot(low, v, (1, 0))
        attn[:, cols] = local + two_term(q, carry_ref[h], (1, 0)) * decay(h, to_carry)

    to_base = jnp.where(
        (pos >= base.astype(F32)) & (begin < base.astype(F32)), pos - (base - 1).astype(F32), inf
    )

    def add_incoming(h, incoming):
        entering = two_term(columns(q_ref, h), incoming, (1, 0)) * decay(h, to_base)
        total = columns(attn, h) + entering
        attn[:, pl.ds(pl.multiple_of(h * width, width), width)] = total
        return total * total

    onward_copies = []
    kept = []
    for i in range(half):
        h = mine + i
        onward[i] = jnp.zeros((width, width), F32)
        for b in range(1, reach + 1):
            @pl.when(receives(b))
            def _():
                layer_copy(b, i).wait_recv()
                steps = 2 * rows * (b - 1)
                onward[i] += factor(h, steps, base_begin <= pair_base - 1 - steps) * landed[b - 1, i]
        before_first = onward[i]
        before_second = pair[0, i] + factor(h, rows, first_begin <= first_last - rows) * before_first
        is_first = y == 0
        onward[i] = jnp.where(is_first, before_second, before_first)
        c = copy(onward.at[i], arrived.at[i], onward_send.at[i], onward_recv.at[i], (partner, g))
        c.start()
        onward_copies.append(c)
        kept.append(jnp.where(is_first, before_first, before_second))
    power = jnp.zeros((rows, width), F32)
    for i in range(half):
        power += add_incoming(mine + i, kept[i])
    for i in range(half):
        onward_copies[i].wait_recv()
        power += add_incoming(other + i, arrived[i])

    ones = jnp.ones((16, width), BF16)
    high, low = split(power)
    squares[...] = (dot(ones, high, (1, 1)) + dot(ones, low, (1, 1)))[:8]
    sq_copies = []
    for j in range(1, n_head):
        c = copy(
            squares, squares_in.at[j - 1], sq_send.at[j - 1], sq_recv.at[j - 1], (d, lax.rem(g + j, n_head))
        )
        c.start()
        sq_copies.append(c)
    total = squares[...]
    for j in range(1, n_head):
        sq_copies[j - 1].wait_recv()
        total = total + squares_in[j - 1]
    scale = lax.rsqrt(total / jnp.float32(features * n_head) + 1e-5)
    scale = jnp.broadcast_to(scale[0:1], (width, rows)).T
    for h in range(heads):
        cols = slice(h * width, (h + 1) * width)
        out_ref[:, cols] = (attn[:, cols] * scale * gain_ref[:, cols]).astype(BF16)

    for c in pair_copies + onward_copies + sq_copies:
        c.wait_send()
    for i in range(half):
        for b in range(1, reach + 1):
            @pl.when(sends(b))
            def _():
                layer_copy(b, i).wait_send()


def shards(queries, key_rows, value_rows, carry_state, decay_rate, norm_gain, order, doc_lengths):
    rows, features = queries.shape
    heads, width, _ = carry_state.shape
    n_ctx, n_head = lax.axis_size("ctx"), lax.axis_size("head")
    longest = min(n_ctx * rows // 2, 2048)
    reach = -(-longest // (2 * rows))
    half = heads // 2
    vmem = pl.BlockSpec(memory_space=pltpu.VMEM)
    smem = pl.BlockSpec(memory_space=pltpu.SMEM)
    dma = pltpu.SemaphoreType.DMA
    return pl.pallas_call(
        functools.partial(kernel, n_ctx, n_head, reach),
        out_shape=jax.ShapeDtypeStruct((rows, features), BF16),
        in_specs=[smem, smem] + [vmem] * 6,
        out_specs=vmem,
        scratch_shapes=[
            pltpu.VMEM((rows, features), F32),
            pltpu.VMEM((2, half, width, width), F32),
            pltpu.VMEM((half, width, width), F32),
            pltpu.VMEM((half, width, width), F32),
            pltpu.VMEM((reach, half, width, width), F32),
            pltpu.VMEM((half, width, width), F32),
            pltpu.VMEM((half, width, width), F32),
            pltpu.VMEM((8, rows), F32),
            pltpu.VMEM((n_head - 1, 8, rows), F32),
            dma((half,)), dma((half,)),
            dma((reach, half)), dma((reach, half)),
            dma((half,)), dma((half,)),
            dma((n_head - 1,)), dma((n_head - 1,)),
        ],
        compiler_params=pltpu.CompilerParams(
            collective_id=0, has_side_effects=True, vmem_limit_bytes=32 * 1024 * 1024
        ),
    )(decay_rate, doc_lengths, queries, key_rows, value_rows, carry_state, norm_gain.reshape(1, features), order)


def solution(mesh):
    return jax.shard_map(
        shards,
        mesh=mesh,
        in_specs=(
            P("ctx", "head"),
            P("ctx", "head"),
            P("ctx", "head"),
            P("head", None, None),
            P("head"),
            P("head"),
            P("ctx", None),
            P(),
        ),
        out_specs=P("ctx", "head"),
        check_vma=False,
    )
```

```python
import functools

import jax
import jax.numpy as jnp
from jax import lax
from jax.experimental import pallas as pl
from jax.experimental.pallas import tpu as pltpu
from jax.sharding import PartitionSpec as P

F32 = jnp.float32
BF16 = jnp.bfloat16
MESH = pl.DeviceIdType.MESH


def split(x):
    high = x.astype(BF16)
    return high, (x - high.astype(F32)).astype(BF16)


def dot(a, b, contract):
    return lax.dot_general(a, b, ((contract[:1], contract[1:]), ((), ())), preferred_element_type=F32)


def two_term(a, b, contract):
    width = b.shape[1]
    both = dot(a, jnp.concatenate(split(b), axis=1), contract)
    return both[:, :width] + both[:, width:]


def kernel(
    n_ctx, n_head, reach,
    rate_hbm, docs_hbm, q_hbm, k_hbm, v_hbm, carry_hbm, gain_hbm, order_hbm, out_ref,
    rate_ref, docs_ref, q_ref, k_ref, v_ref, carry_ref, gain_ref, order_ref, load_sem,
    attn, pair, away, layer, landed, onward, arrived, squares, squares_in,
    pair_send, pair_recv, layer_send, layer_recv, onward_send, onward_recv, sq_send, sq_recv,
):
    rows, features = q_ref.shape
    heads = rate_ref.shape[0]
    width = features // heads
    half = heads // 2
    n_docs = docs_ref.shape[0]
    spill = rows // 4
    keep = rows - spill
    tokens = n_ctx * rows
    n_pairs = n_ctx // 2
    d = lax.axis_index("ctx")
    g = lax.axis_index("head")
    u = d // 2
    y = lax.rem(d, 2)
    partner = d + 1 - 2 * y
    mine = y * half
    other = (1 - y) * half

    def sends(b):
        return u + b <= n_pairs

    def receives(b):
        return (u >= b) | (u == 0)

    loads = {}
    operands = (
        (order_hbm, order_ref), (docs_hbm, docs_ref), (rate_hbm, rate_ref), (v_hbm, v_ref),
        (k_hbm, k_ref), (q_hbm, q_ref), (carry_hbm, carry_ref), (gain_hbm, gain_ref),
    )
    for n, (source, held) in enumerate(operands):
        loads[id(held)] = pltpu.make_async_copy(source, held, load_sem.at[n])
        loads[id(held)].start()

    barrier = pltpu.get_barrier_semaphore()
    pl.semaphore_signal(barrier, inc=1, device_id=(partner, g), device_id_type=MESH)
    for j in range(1, n_head):
        pl.semaphore_signal(
            barrier, inc=1, device_id=(d, lax.rem(g + n_head - j, n_head)), device_id_type=MESH
        )
    expected = jnp.int32(n_head)
    for b in range(1, reach + 1):
        @pl.when(receives(b))
        def _():
            source = lax.rem(u + n_pairs - b, n_pairs) * 2 + y
            pl.semaphore_signal(barrier, inc=1, device_id=(source, g), device_id_type=MESH)
        expected = expected + sends(b).astype(jnp.int32)

    for held in (order_ref, docs_ref, rate_ref):
        loads[id(held)].wait()

    base = jnp.where(d == 0, tokens, d * rows) - spill
    last = d * rows + keep - 1
    chosen = (order_ref[...] == lax.broadcasted_iota(jnp.int32, (rows, rows), 0)).astype(F32).astype(BF16)
    index = lax.broadcasted_iota(jnp.int32, (rows, rows), 0).astype(F32).astype(BF16)
    along = lax.broadcasted_iota(jnp.int32, (16, rows), 1).astype(F32).astype(BF16)

    def position(slot):
        kept_at = (d * rows).astype(F32)
        moved_at = (base - keep).astype(F32)
        return slot + jnp.where(slot < keep, kept_at, moved_at)

    down = position(dot(chosen, index, (1, 0)))
    across = position(dot(along, chosen, (1, 1)))[0:1]
    pos = down[:, :width]

    pair_last = 2 * u * rows + rows + keep - 1
    first_last = 2 * u * rows + keep - 1
    pair_base = jnp.where(u == 0, tokens, 2 * u * rows) - spill
    marks = (last, pair_last, first_last, pair_base - 1)

    def document(n, carried):
        edge, begin, scalars = carried
        edge = edge + docs_ref[n]
        mark = edge.astype(F32)
        begin = jnp.where(pos >= mark, mark, begin)
        return edge, begin, tuple(jnp.where(m >= edge, edge, s) for m, s in zip(marks, scalars))

    zero = jnp.int32(0)
    state = (zero, jnp.zeros((rows, width), F32), (zero,) * 4)
    if n_docs <= 32:
        for n in range(n_docs):
            state = document(n, state)
    else:
        state = lax.fori_loop(0, n_docs, document, state)
    _, begin, (last_begin, pair_begin, first_begin, base_begin) = state

    inf = jnp.float32(jnp.inf)

    def decay(h, steps):
        return jnp.exp(-rate_ref[h] * steps)

    def factor(h, steps, holds):
        return decay(h, jnp.full((1, width), jnp.where(holds, jnp.float32(steps), inf)))

    def columns(ref, h):
        return ref[:, pl.ds(pl.multiple_of(h * width, width), width)]

    to_last = jnp.where((pos <= last.astype(F32)) & (pos >= last_begin.astype(F32)), last.astype(F32) - pos, inf)

    def own_state(h):
        weighted = columns(v_ref, h).astype(F32) * decay(h, to_last)
        return two_term(columns(k_ref, h), weighted, (0, 0))

    def copy(src, dst, send, recv, target):
        return pltpu.make_async_remote_copy(
            src_ref=src, dst_ref=dst, send_sem=send, recv_sem=recv, device_id=target, device_id_type=MESH
        )

    loads[id(v_ref)].wait()
    loads[id(k_ref)].wait()

    pair_copies = []
    for i in range(half):
        away[i] = own_state(other + i)
        if i == 0:
            pl.semaphore_wait(barrier, expected)
        c = copy(away.at[i], pair.at[y, i], pair_send.at[i], pair_recv.at[i], (partner, g))
        c.start()
        pair_copies.append(c)
    for i in range(half):
        pair[y, i] = own_state(mine + i)

    def layer_copy(b, i):
        target = lax.rem(u + b, n_pairs) * 2 + y
        return copy(layer.at[i], landed.at[b - 1, i], layer_send.at[b - 1, i], layer_recv.at[b - 1, i], (target, g))

    for i in range(half):
        pair_copies[i].wait_recv()
        layer[i] = pair[1, i] + factor(mine + i, rows, pair_begin <= pair_last - rows) * pair[0, i]
        for b in range(1, reach + 1):
            @pl.when(sends(b))
            def _():
                layer_copy(b, i).start()

    gap = down - across
    begins = jnp.concatenate([begin] * (rows // width), axis=1)
    gap = jnp.where((gap >= 0) & (across >= begins), gap, inf)
    to_carry = jnp.where(begin == 0, pos + 1, inf)
    loads[id(q_ref)].wait()
    loads[id(carry_ref)].wait()
    for h in range(heads):
        cols = slice(h * width, (h + 1) * width)
        q, v = q_ref[:, cols], v_ref[:, cols]
        weights = dot(q, k_ref[:, cols], (1, 1)) * decay(h, gap)
        high, low = split(weights)
        local = dot(high, v, (1, 0)) + dot(low, v, (1, 0))
        attn[:, cols] = local + two_term(q, carry_ref[h], (1, 0)) * decay(h, to_carry)

    to_base = jnp.where(
        (pos >= base.astype(F32)) & (begin < base.astype(F32)), pos - (base - 1).astype(F32), inf
    )

    def add_incoming(h, incoming):
        entering = two_term(columns(q_ref, h), incoming, (1, 0)) * decay(h, to_base)
        total = columns(attn, h) + entering
        attn[:, pl.ds(pl.multiple_of(h * width, width), width)] = total
        return total * total

    onward_copies = []
    kept = []
    for i in range(half):
        h = mine + i
        onward[i] = jnp.zeros((width, width), F32)
        for b in range(1, reach + 1):
            @pl.when(receives(b))
            def _():
                layer_copy(b, i).wait_recv()
                steps = 2 * rows * (b - 1)
                onward[i] += factor(h, steps, base_begin <= pair_base - 1 - steps) * landed[b - 1, i]
        before_first = onward[i]
        before_second = pair[0, i] + factor(h, rows, first_begin <= first_last - rows) * before_first
        is_first = y == 0
        onward[i] = jnp.where(is_first, before_second, before_first)
        c = copy(onward.at[i], arrived.at[i], onward_send.at[i], onward_recv.at[i], (partner, g))
        c.start()
        onward_copies.append(c)
        kept.append(jnp.where(is_first, before_first, before_second))
    power = jnp.zeros((rows, width), F32)
    for i in range(half):
        power += add_incoming(mine + i, kept[i])
    for i in range(half):
        onward_copies[i].wait_recv()
        power += add_incoming(other + i, arrived[i])

    ones = jnp.ones((16, width), BF16)
    high, low = split(power)
    squares[...] = (dot(ones, high, (1, 1)) + dot(ones, low, (1, 1)))[:8]
    sq_copies = []
    for j in range(1, n_head):
        c = copy(
            squares, squares_in.at[j - 1], sq_send.at[j - 1], sq_recv.at[j - 1], (d, lax.rem(g + j, n_head))
        )
        c.start()
        sq_copies.append(c)
    total = squares[...]
    for j in range(1, n_head):
        sq_copies[j - 1].wait_recv()
        total = total + squares_in[j - 1]
    scale = lax.rsqrt(total / jnp.float32(features * n_head) + 1e-5)
    scale = jnp.broadcast_to(scale[0:1], (width, rows)).T
    loads[id(gain_ref)].wait()
    for h in range(heads):
        cols = slice(h * width, (h + 1) * width)
        out_ref[:, cols] = (attn[:, cols] * scale * gain_ref[:, cols]).astype(BF16)

    for c in pair_copies + onward_copies + sq_copies:
        c.wait_send()
    for i in range(half):
        for b in range(1, reach + 1):
            @pl.when(sends(b))
            def _():
                layer_copy(b, i).wait_send()


def shards(queries, key_rows, value_rows, carry_state, decay_rate, norm_gain, order, doc_lengths):
    rows, features = queries.shape
    heads, width, _ = carry_state.shape
    n_ctx, n_head = lax.axis_size("ctx"), lax.axis_size("head")
    longest = min(n_ctx * rows // 2, 2048)
    reach = -(-longest // (2 * rows))
    half = heads // 2
    vmem = pl.BlockSpec(memory_space=pltpu.VMEM)
    hbm = pl.BlockSpec(memory_space=pltpu.HBM)
    dma = pltpu.SemaphoreType.DMA
    return pl.pallas_call(
        functools.partial(kernel, n_ctx, n_head, reach),
        out_shape=jax.ShapeDtypeStruct((rows, features), BF16),
        in_specs=[hbm] * 8,
        out_specs=vmem,
        scratch_shapes=[
            pltpu.SMEM(decay_rate.shape, F32),
            pltpu.SMEM(doc_lengths.shape, jnp.int32),
            pltpu.VMEM((rows, features), BF16),
            pltpu.VMEM((rows, features), BF16),
            pltpu.VMEM((rows, features), BF16),
            pltpu.VMEM(carry_state.shape, F32),
            pltpu.VMEM((1, features), F32),
            pltpu.VMEM(order.shape, jnp.int32),
            dma((8,)),
            pltpu.VMEM((rows, features), F32),
            pltpu.VMEM((2, half, width, width), F32),
            pltpu.VMEM((half, width, width), F32),
            pltpu.VMEM((half, width, width), F32),
            pltpu.VMEM((reach, half, width, width), F32),
            pltpu.VMEM((half, width, width), F32),
            pltpu.VMEM((half, width, width), F32),
            pltpu.VMEM((8, rows), F32),
            pltpu.VMEM((n_head - 1, 8, rows), F32),
            dma((half,)), dma((half,)),
            dma((reach, half)), dma((reach, half)),
            dma((half,)), dma((half,)),
            dma((n_head - 1,)), dma((n_head - 1,)),
        ],
        compiler_params=pltpu.CompilerParams(
            collective_id=0, has_side_effects=True, vmem_limit_bytes=64 * 1024 * 1024
        ),
    )(decay_rate, doc_lengths, queries, key_rows, value_rows, carry_state, norm_gain.reshape(1, features), order)


def solution(mesh):
    return jax.shard_map(
        shards,
        mesh=mesh,
        in_specs=(
            P("ctx", "head"),
            P("ctx", "head"),
            P("ctx", "head"),
            P("head", None, None),
            P("head"),
            P("head"),
            P("ctx", None),
            P(),
        ),
        out_specs=P("ctx", "head"),
        check_vma=False,
    )
```

```python
import functools

import jax
import jax.numpy as jnp
from jax import lax
from jax.experimental import pallas as pl
from jax.experimental.pallas import tpu as pltpu
from jax.sharding import PartitionSpec as P

F32 = jnp.float32
BF16 = jnp.bfloat16
MESH = pl.DeviceIdType.MESH


def split(x):
    high = x.astype(BF16)
    return high, (x - high.astype(F32)).astype(BF16)


def dot(a, b, contract):
    return lax.dot_general(a, b, ((contract[:1], contract[1:]), ((), ())), preferred_element_type=F32)


def two_term(a, b, contract):
    width = b.shape[1]
    both = dot(a, jnp.concatenate(split(b), axis=1), contract)
    return both[:, :width] + both[:, width:]


def coded(x):
    top = jnp.maximum(jnp.max(jnp.abs(x), axis=0, keepdims=True), 1e-30)
    level = jnp.ceil(jnp.log2(top) * 16.0)
    counts = jnp.round(x * (jnp.exp2(level * -0.0625) * 32760.0))
    rows = jnp.concatenate([counts, jnp.broadcast_to(level, (16, x.shape[1]))], axis=0)
    return rows.astype(jnp.int32).astype(jnp.int16)


def decoded(ref, index):
    whole = ref[index].astype(jnp.int32).astype(F32)
    width = whole.shape[1]
    return whole[:width] * (jnp.exp2(whole[width : width + 1] * 0.0625) * (1.0 / 32760.0))


def kernel(
    n_ctx, n_head, reach,
    rate_hbm, docs_hbm, q_hbm, k_hbm, v_hbm, carry_hbm, gain_hbm, order_hbm, out_ref,
    rate_ref, docs_ref, q_ref, k_ref, v_ref, carry_ref, gain_ref, order_ref, load_sem,
    attn, pair, pair_in, away, layer, landed, entering, onward, arrived, squares, squares_in,
    pair_send, pair_recv, layer_send, layer_recv, onward_send, onward_recv, sq_send, sq_recv,
):
    rows, features = q_ref.shape
    heads = rate_ref.shape[0]
    width = features // heads
    half = heads // 2
    n_docs = docs_ref.shape[0]
    spill = rows // 4
    keep = rows - spill
    tokens = n_ctx * rows
    n_pairs = n_ctx // 2
    d = lax.axis_index("ctx")
    g = lax.axis_index("head")
    u = d // 2
    y = lax.rem(d, 2)
    partner = d + 1 - 2 * y
    mine = y * half
    other = (1 - y) * half

    def sends(b):
        return u + b <= n_pairs

    def receives(b):
        return (u >= b) | (u == 0)

    loads = {}
    operands = (
        (order_hbm, order_ref), (docs_hbm, docs_ref), (rate_hbm, rate_ref), (v_hbm, v_ref),
        (k_hbm, k_ref), (q_hbm, q_ref), (carry_hbm, carry_ref), (gain_hbm, gain_ref),
    )
    for n, (source, held) in enumerate(operands):
        loads[id(held)] = pltpu.make_async_copy(source, held, load_sem.at[n])
        loads[id(held)].start()

    barrier = pltpu.get_barrier_semaphore()
    pl.semaphore_signal(barrier, inc=1, device_id=(partner, g), device_id_type=MESH)
    for j in range(1, n_head):
        pl.semaphore_signal(
            barrier, inc=1, device_id=(d, lax.rem(g + n_head - j, n_head)), device_id_type=MESH
        )
    expected = jnp.int32(n_head)
    for b in range(1, reach + 1):
        @pl.when(receives(b))
        def _():
            source = lax.rem(u + n_pairs - b, n_pairs) * 2 + y
            pl.semaphore_signal(barrier, inc=1, device_id=(source, g), device_id_type=MESH)
        expected = expected + sends(b).astype(jnp.int32)

    for held in (order_ref, docs_ref, rate_ref):
        loads[id(held)].wait()

    base = jnp.where(d == 0, tokens, d * rows) - spill
    last = d * rows + keep - 1
    chosen = (order_ref[...] == lax.broadcasted_iota(jnp.int32, (rows, rows), 0)).astype(F32).astype(BF16)
    index = lax.broadcasted_iota(jnp.int32, (rows, rows), 0).astype(F32).astype(BF16)
    along = lax.broadcasted_iota(jnp.int32, (16, rows), 1).astype(F32).astype(BF16)

    def position(slot):
        kept_at = (d * rows).astype(F32)
        moved_at = (base - keep).astype(F32)
        return slot + jnp.where(slot < keep, kept_at, moved_at)

    down = position(dot(chosen, index, (1, 0)))
    across = position(dot(along, chosen, (1, 1)))[0:1]
    pos = down[:, :width]

    pair_last = 2 * u * rows + rows + keep - 1
    first_last = 2 * u * rows + keep - 1
    pair_base = jnp.where(u == 0, tokens, 2 * u * rows) - spill
    marks = (last, pair_last, first_last, pair_base - 1)

    def over_documents(step, state):
        if n_docs <= 32:
            for n in range(n_docs):
                state = step(n, state)
            return state
        return lax.fori_loop(0, n_docs, step, state)

    def scalar_starts(n, carried):
        edge, starts = carried
        edge = edge + docs_ref[n]
        return edge, tuple(jnp.where(m >= edge, edge, s) for m, s in zip(marks, starts))

    def row_starts(n, carried):
        edge, begin = carried
        edge = edge + docs_ref[n]
        mark = edge.astype(F32)
        return edge, jnp.where(pos >= mark, mark, begin)

    zero = jnp.int32(0)
    last_begin, pair_begin, first_begin, base_begin = over_documents(scalar_starts, (zero, (zero,) * 4))[1]

    inf = jnp.float32(jnp.inf)

    def decay(h, steps):
        return jnp.exp(-rate_ref[h] * steps)

    def factor(h, steps, holds):
        return decay(h, jnp.full((1, width), jnp.where(holds, jnp.float32(steps), inf)))

    def columns(ref, h):
        return ref[:, pl.ds(pl.multiple_of(h * width, width), width)]

    to_last = jnp.where((pos <= last.astype(F32)) & (pos >= last_begin.astype(F32)), last.astype(F32) - pos, inf)

    def own_state(h):
        weighted = columns(v_ref, h).astype(F32) * decay(h, to_last)
        return two_term(columns(k_ref, h), weighted, (0, 0))

    def copy(src, dst, send, recv, target):
        return pltpu.make_async_remote_copy(
            src_ref=src, dst_ref=dst, send_sem=send, recv_sem=recv, device_id=target, device_id_type=MESH
        )

    loads[id(v_ref)].wait()
    loads[id(k_ref)].wait()

    pair_copies = []
    for i in range(half):
        away[i] = coded(own_state(other + i))
        if i == 0:
            pl.semaphore_wait(barrier, expected)
        c = copy(away.at[i], pair_in.at[i], pair_send.at[i], pair_recv.at[i], (partner, g))
        c.start()
        pair_copies.append(c)
    for i in range(half):
        pair[i] = own_state(mine + i)

    begin = over_documents(row_starts, (zero, jnp.zeros((rows, width), F32)))[1]
    gap = down - across
    begins = jnp.concatenate([begin] * (rows // width), axis=1)
    gap = jnp.where((gap >= 0) & (across >= begins), gap, inf)
    to_carry = jnp.where(begin == 0, pos + 1, inf)
    to_base = jnp.where(
        (pos >= base.astype(F32)) & (begin < base.astype(F32)), pos - (base - 1).astype(F32), inf
    )

    def add_local(h):
        cols = slice(h * width, (h + 1) * width)
        q, v = q_ref[:, cols], v_ref[:, cols]
        weights = dot(q, k_ref[:, cols], (1, 1)) * decay(h, gap)
        high, low = split(weights)
        local = dot(high, v, (1, 0)) + dot(low, v, (1, 0))
        attn[:, cols] = local + two_term(q, carry_ref[h], (1, 0)) * decay(h, to_carry)

    loads[id(q_ref)].wait()
    loads[id(carry_ref)].wait()

    def layer_copy(b, i):
        target = lax.rem(u + b, n_pairs) * 2 + y
        return copy(layer.at[i], landed.at[b - 1, i], layer_send.at[b - 1, i], layer_recv.at[b - 1, i], (target, g))

    is_first = y == 0
    for i in range(half):
        pair_copies[i].wait_recv()
        theirs, ours = decoded(pair_in, i), pair[i]
        first = jnp.where(is_first, ours, theirs)
        second = jnp.where(is_first, theirs, ours)
        layer[i] = coded(second + factor(mine + i, rows, pair_begin <= pair_last - rows) * first)
        pair[i] = first
        for b in range(1, reach + 1):
            @pl.when(sends(b))
            def _():
                layer_copy(b, i).start()
    for h in range(heads):
        add_local(h)

    def add_incoming(h, incoming):
        total = columns(attn, h) + two_term(columns(q_ref, h), incoming, (1, 0)) * decay(h, to_base)
        attn[:, pl.ds(pl.multiple_of(h * width, width), width)] = total
        return total * total

    onward_copies = []
    kept = []
    for i in range(half):
        h = mine + i
        entering[i] = jnp.zeros((width, width), F32)
        for b in range(1, reach + 1):
            @pl.when(receives(b))
            def _():
                layer_copy(b, i).wait_recv()
                steps = 2 * rows * (b - 1)
                fade = factor(h, steps, base_begin <= pair_base - 1 - steps)
                entering[i] += fade * decoded(landed, (b - 1, i))
        before_first = entering[i]
        before_second = pair[i] + factor(h, rows, first_begin <= first_last - rows) * before_first
        onward[i] = coded(jnp.where(is_first, before_second, before_first))
        c = copy(onward.at[i], arrived.at[i], onward_send.at[i], onward_recv.at[i], (partner, g))
        c.start()
        onward_copies.append(c)
        kept.append(jnp.where(is_first, before_first, before_second))
    power = jnp.zeros((rows, width), F32)
    for i in range(half):
        power += add_incoming(mine + i, kept[i])
    for i in range(half):
        onward_copies[i].wait_recv()
        power += add_incoming(other + i, decoded(arrived, i))

    ones = jnp.ones((16, width), BF16)
    high, low = split(power)
    squares[...] = (dot(ones, high, (1, 1)) + dot(ones, low, (1, 1)))[:8]
    sq_copies = []
    for j in range(1, n_head):
        c = copy(
            squares, squares_in.at[j - 1], sq_send.at[j - 1], sq_recv.at[j - 1], (d, lax.rem(g + j, n_head))
        )
        c.start()
        sq_copies.append(c)
    total = squares[...]
    for j in range(1, n_head):
        sq_copies[j - 1].wait_recv()
        total = total + squares_in[j - 1]
    scale = lax.rsqrt(total / jnp.float32(features * n_head) + 1e-5)
    scale = jnp.broadcast_to(scale[0:1], (width, rows)).T
    loads[id(gain_ref)].wait()
    for h in range(heads):
        cols = slice(h * width, (h + 1) * width)
        out_ref[:, cols] = (attn[:, cols] * scale * gain_ref[:, cols]).astype(BF16)

    for c in pair_copies + onward_copies + sq_copies:
        c.wait_send()
    for i in range(half):
        for b in range(1, reach + 1):
            @pl.when(sends(b))
            def _():
                layer_copy(b, i).wait_send()


def shards(queries, key_rows, value_rows, carry_state, decay_rate, norm_gain, order, doc_lengths):
    rows, features = queries.shape
    heads, width, _ = carry_state.shape
    n_ctx, n_head = lax.axis_size("ctx"), lax.axis_size("head")
    longest = min(n_ctx * rows // 2, 2048)
    reach = -(-longest // (2 * rows))
    half = heads // 2
    vmem = pl.BlockSpec(memory_space=pltpu.VMEM)
    hbm = pl.BlockSpec(memory_space=pltpu.HBM)
    dma = pltpu.SemaphoreType.DMA
    return pl.pallas_call(
        functools.partial(kernel, n_ctx, n_head, reach),
        out_shape=jax.ShapeDtypeStruct((rows, features), BF16),
        in_specs=[hbm] * 8,
        out_specs=vmem,
        scratch_shapes=[
            pltpu.SMEM(decay_rate.shape, F32),
            pltpu.SMEM(doc_lengths.shape, jnp.int32),
            pltpu.VMEM((rows, features), BF16),
            pltpu.VMEM((rows, features), BF16),
            pltpu.VMEM((rows, features), BF16),
            pltpu.VMEM(carry_state.shape, F32),
            pltpu.VMEM((1, features), F32),
            pltpu.VMEM(order.shape, jnp.int32),
            dma((8,)),
            pltpu.VMEM((rows, features), F32),
            pltpu.VMEM((half, width, width), F32),
            pltpu.VMEM((half, width + 16, width), jnp.int16),
            pltpu.VMEM((half, width + 16, width), jnp.int16),
            pltpu.VMEM((half, width + 16, width), jnp.int16),
            pltpu.VMEM((reach, half, width + 16, width), jnp.int16),
            pltpu.VMEM((half, width, width), F32),
            pltpu.VMEM((half, width + 16, width), jnp.int16),
            pltpu.VMEM((half, width + 16, width), jnp.int16),
            pltpu.VMEM((8, rows), F32),
            pltpu.VMEM((n_head - 1, 8, rows), F32),
            dma((half,)), dma((half,)),
            dma((reach, half)), dma((reach, half)),
            dma((half,)), dma((half,)),
            dma((n_head - 1,)), dma((n_head - 1,)),
        ],
        compiler_params=pltpu.CompilerParams(
            collective_id=0, has_side_effects=True, vmem_limit_bytes=64 * 1024 * 1024
        ),
    )(decay_rate, doc_lengths, queries, key_rows, value_rows, carry_state, norm_gain.reshape(1, features), order)


def solution(mesh):
    return jax.shard_map(
        shards,
        mesh=mesh,
        in_specs=(
            P("ctx", "head"),
            P("ctx", "head"),
            P("ctx", "head"),
            P("head", None, None),
            P("head"),
            P("head"),
            P("ctx", None),
            P(),
        ),
        out_specs=P("ctx", "head"),
        check_vma=False,
    )
```

```python
import functools

import jax
import jax.numpy as jnp
from jax import lax
from jax.experimental import pallas as pl
from jax.experimental.pallas import tpu as pltpu
from jax.sharding import PartitionSpec as P

F32 = jnp.float32
BF16 = jnp.bfloat16
MESH = pl.DeviceIdType.MESH


def split(x):
    high = x.astype(BF16)
    return high, (x - high.astype(F32)).astype(BF16)


def dot(a, b, contract):
    return lax.dot_general(a, b, ((contract[:1], contract[1:]), ((), ())), preferred_element_type=F32)


def two_term(a, b, contract):
    width = b.shape[1]
    both = dot(a, jnp.concatenate(split(b), axis=1), contract)
    return both[:, :width] + both[:, width:]


def coded(x):
    top = jnp.maximum(jnp.max(jnp.abs(x), axis=0, keepdims=True), 1e-30)
    level = jnp.ceil(jnp.log2(top) * 16.0)
    counts = jnp.round(x * (jnp.exp2(level * -0.0625) * 32760.0))
    rows = jnp.concatenate([counts, jnp.broadcast_to(level, (16, x.shape[1]))], axis=0)
    return rows.astype(jnp.int32).astype(jnp.int16)


def decoded(ref, index):
    whole = ref[index].astype(jnp.int32).astype(F32)
    width = whole.shape[1]
    return whole[:width] * (jnp.exp2(whole[width : width + 1] * 0.0625) * (1.0 / 32760.0))


def kernel(
    n_ctx, n_head, reach,
    rate_hbm, docs_hbm, q_hbm, k_hbm, v_hbm, carry_hbm, gain_hbm, order_hbm, out_ref,
    rate_ref, docs_ref, q_ref, k_ref, v_ref, carry_ref, gain_ref, order_ref, load_sem,
    attn, pair, pair_in, away, layer, landed, entering, onward, arrived, squares, squares_in,
    pair_send, pair_recv, layer_send, layer_recv, wrap_send, onward_send, onward_recv, sq_send, sq_recv,
):
    rows, features = q_ref.shape
    heads = rate_ref.shape[0]
    width = features // heads
    half = heads // 2
    n_docs = docs_ref.shape[0]
    spill = rows // 4
    keep = rows - spill
    tokens = n_ctx * rows
    n_pairs = n_ctx // 2
    d = lax.axis_index("ctx")
    g = lax.axis_index("head")
    u = d // 2
    y = lax.rem(d, 2)
    partner = d + 1 - 2 * y
    mine = y * half
    other = (1 - y) * half

    inner = u + 1 < n_pairs

    def forwards(b):
        return inner & (u >= b - 1)

    def wraps(b):
        return u == n_pairs - b

    def receives(b):
        return (u >= b) | (u == 0)

    loads = {}
    operands = (
        (order_hbm, order_ref), (docs_hbm, docs_ref), (rate_hbm, rate_ref), (v_hbm, v_ref),
        (k_hbm, k_ref), (q_hbm, q_ref), (carry_hbm, carry_ref), (gain_hbm, gain_ref),
    )
    for n, (source, held) in enumerate(operands):
        loads[id(held)] = pltpu.make_async_copy(source, held, load_sem.at[n])
        loads[id(held)].start()

    barrier = pltpu.get_barrier_semaphore()
    pl.semaphore_signal(barrier, inc=1, device_id=(partner, g), device_id_type=MESH)
    for j in range(1, n_head):
        pl.semaphore_signal(
            barrier, inc=1, device_id=(d, lax.rem(g + n_head - j, n_head)), device_id_type=MESH
        )

    @pl.when(u > 0)
    def _():
        pl.semaphore_signal(barrier, inc=1, device_id=(d - 2, g), device_id_type=MESH)
    expected = n_head + inner.astype(jnp.int32)
    for b in range(1, reach + 1):
        @pl.when(u == 0)
        def _():
            pl.semaphore_signal(barrier, inc=1, device_id=(2 * (n_pairs - b) + y, g), device_id_type=MESH)
        expected = expected + wraps(b).astype(jnp.int32)

    for held in (order_ref, docs_ref, rate_ref):
        loads[id(held)].wait()

    base = jnp.where(d == 0, tokens, d * rows) - spill
    last = d * rows + keep - 1
    chosen = (order_ref[...] == lax.broadcasted_iota(jnp.int32, (rows, rows), 0)).astype(F32).astype(BF16)
    index = lax.broadcasted_iota(jnp.int32, (rows, rows), 0).astype(F32).astype(BF16)
    along = lax.broadcasted_iota(jnp.int32, (16, rows), 1).astype(F32).astype(BF16)

    def position(slot):
        kept_at = (d * rows).astype(F32)
        moved_at = (base - keep).astype(F32)
        return slot + jnp.where(slot < keep, kept_at, moved_at)

    down = position(dot(chosen, index, (1, 0)))
    across = position(dot(along, chosen, (1, 1)))[0:1]
    pos = down[:, :width]

    pair_last = 2 * u * rows + rows + keep - 1
    first_last = 2 * u * rows + keep - 1
    pair_base = jnp.where(u == 0, tokens, 2 * u * rows) - spill
    marks = (last, pair_last, first_last, pair_base - 1)

    def over_documents(step, state):
        if n_docs <= 32:
            for n in range(n_docs):
                state = step(n, state)
            return state
        return lax.fori_loop(0, n_docs, step, state)

    def scalar_starts(n, carried):
        edge, starts = carried
        edge = edge + docs_ref[n]
        return edge, tuple(jnp.where(m >= edge, edge, s) for m, s in zip(marks, starts))

    def row_starts(n, carried):
        edge, begin = carried
        edge = edge + docs_ref[n]
        mark = edge.astype(F32)
        return edge, jnp.where(pos >= mark, mark, begin)

    zero = jnp.int32(0)
    last_begin, pair_begin, first_begin, base_begin = over_documents(scalar_starts, (zero, (zero,) * 4))[1]

    inf = jnp.float32(jnp.inf)

    def decay(h, steps):
        return jnp.exp(-rate_ref[h] * steps)

    def factor(h, steps, holds):
        return decay(h, jnp.full((1, width), jnp.where(holds, jnp.float32(steps), inf)))

    def columns(ref, h):
        return ref[:, pl.ds(pl.multiple_of(h * width, width), width)]

    to_last = jnp.where((pos <= last.astype(F32)) & (pos >= last_begin.astype(F32)), last.astype(F32) - pos, inf)

    def own_state(h):
        weighted = columns(v_ref, h).astype(F32) * decay(h, to_last)
        return two_term(columns(k_ref, h), weighted, (0, 0))

    def copy(src, dst, send, recv, target):
        return pltpu.make_async_remote_copy(
            src_ref=src, dst_ref=dst, send_sem=send, recv_sem=recv, device_id=target, device_id_type=MESH
        )

    loads[id(v_ref)].wait()
    loads[id(k_ref)].wait()

    pair_copies = []
    for i in range(half):
        away[i] = coded(own_state(other + i))
        if i == 0:
            pl.semaphore_wait(barrier, expected)
        c = copy(away.at[i], pair_in.at[i], pair_send.at[i], pair_recv.at[i], (partner, g))
        c.start()
        pair_copies.append(c)
    for i in range(half):
        pair[i] = own_state(mine + i)

    begin = over_documents(row_starts, (zero, jnp.zeros((rows, width), F32)))[1]
    gap = down - across
    begins = jnp.concatenate([begin] * (rows // width), axis=1)
    gap = jnp.where((gap >= 0) & (across >= begins), gap, inf)
    to_carry = jnp.where(begin == 0, pos + 1, inf)
    to_base = jnp.where(
        (pos >= base.astype(F32)) & (begin < base.astype(F32)), pos - (base - 1).astype(F32), inf
    )

    def add_local(h):
        cols = slice(h * width, (h + 1) * width)
        q, v = q_ref[:, cols], v_ref[:, cols]
        weights = dot(q, k_ref[:, cols], (1, 1)) * decay(h, gap)
        high, low = split(weights)
        local = dot(high, v, (1, 0)) + dot(low, v, (1, 0))
        attn[:, cols] = local + two_term(q, carry_ref[h], (1, 0)) * decay(h, to_carry)

    loads[id(q_ref)].wait()
    loads[id(carry_ref)].wait()

    def forward_copy(b, i):
        source = layer.at[i] if b == 1 else landed.at[b - 2, i]
        target = lax.rem(d + 2, n_ctx)
        return copy(source, landed.at[b - 1, i], layer_send.at[b - 1, i], layer_recv.at[b - 1, i], (target, g))

    def wrap_copy(b, i):
        return copy(layer.at[i], landed.at[b - 1, i], wrap_send.at[i], layer_recv.at[b - 1, i], (y, g))

    def forward(b, i):
        @pl.when(u >= b - 1)
        def _():
            forward_copy(b - 1, i).wait_recv()

        @pl.when(forwards(b))
        def _():
            forward_copy(b, i).start()

    is_first = y == 0
    for i in range(half):
        pair_copies[i].wait_recv()
        theirs, ours = decoded(pair_in, i), pair[i]
        first = jnp.where(is_first, ours, theirs)
        second = jnp.where(is_first, theirs, ours)
        layer[i] = coded(second + factor(mine + i, rows, pair_begin <= pair_last - rows) * first)
        pair[i] = first
        @pl.when(forwards(1))
        def _():
            forward_copy(1, i).start()
        for b in range(1, reach + 1):
            @pl.when(wraps(b))
            def _():
                wrap_copy(b, i).start()
    hops = [(b, i) for b in range(2, reach + 1) for i in range(half)]
    for h in range(heads):
        add_local(h)
        if h >= 1 and hops:
            forward(*hops.pop(0))
    for hop in hops:
        forward(*hop)

    def add_incoming(h, incoming):
        total = columns(attn, h) + two_term(columns(q_ref, h), incoming, (1, 0)) * decay(h, to_base)
        attn[:, pl.ds(pl.multiple_of(h * width, width), width)] = total
        return total * total

    onward_copies = []
    kept = []
    for i in range(half):
        h = mine + i
        entering[i] = jnp.zeros((width, width), F32)
        for b in range(1, reach + 1):
            @pl.when(receives(b))
            def _():
                @pl.when((u == 0) | (b == reach))
                def _():
                    forward_copy(b, i).wait_recv()

                steps = 2 * rows * (b - 1)
                fade = factor(h, steps, base_begin <= pair_base - 1 - steps)
                entering[i] += fade * decoded(landed, (b - 1, i))
        before_first = entering[i]
        before_second = pair[i] + factor(h, rows, first_begin <= first_last - rows) * before_first
        onward[i] = coded(jnp.where(is_first, before_second, before_first))
        c = copy(onward.at[i], arrived.at[i], onward_send.at[i], onward_recv.at[i], (partner, g))
        c.start()
        onward_copies.append(c)
        kept.append(jnp.where(is_first, before_first, before_second))
    power = jnp.zeros((rows, width), F32)
    for i in range(half):
        power += add_incoming(mine + i, kept[i])
    for i in range(half):
        onward_copies[i].wait_recv()
        power += add_incoming(other + i, decoded(arrived, i))

    ones = jnp.ones((16, width), BF16)
    high, low = split(power)
    squares[...] = (dot(ones, high, (1, 1)) + dot(ones, low, (1, 1)))[:8]
    sq_copies = []
    for j in range(1, n_head):
        c = copy(
            squares, squares_in.at[j - 1], sq_send.at[j - 1], sq_recv.at[j - 1], (d, lax.rem(g + j, n_head))
        )
        c.start()
        sq_copies.append(c)
    total = squares[...]
    for j in range(1, n_head):
        sq_copies[j - 1].wait_recv()
        total = total + squares_in[j - 1]
    scale = lax.rsqrt(total / jnp.float32(features * n_head) + 1e-5)
    scale = jnp.broadcast_to(scale[0:1], (width, rows)).T
    loads[id(gain_ref)].wait()
    for h in range(heads):
        cols = slice(h * width, (h + 1) * width)
        out_ref[:, cols] = (attn[:, cols] * scale * gain_ref[:, cols]).astype(BF16)

    for c in pair_copies + onward_copies + sq_copies:
        c.wait_send()
    for i in range(half):
        for b in range(1, reach + 1):
            @pl.when(forwards(b))
            def _():
                forward_copy(b, i).wait_send()

            @pl.when(wraps(b))
            def _():
                wrap_copy(b, i).wait_send()


def shards(queries, key_rows, value_rows, carry_state, decay_rate, norm_gain, order, doc_lengths):
    rows, features = queries.shape
    heads, width, _ = carry_state.shape
    n_ctx, n_head = lax.axis_size("ctx"), lax.axis_size("head")
    longest = min(n_ctx * rows // 2, 2048)
    reach = -(-longest // (2 * rows))
    half = heads // 2
    vmem = pl.BlockSpec(memory_space=pltpu.VMEM)
    hbm = pl.BlockSpec(memory_space=pltpu.HBM)
    dma = pltpu.SemaphoreType.DMA
    return pl.pallas_call(
        functools.partial(kernel, n_ctx, n_head, reach),
        out_shape=jax.ShapeDtypeStruct((rows, features), BF16),
        in_specs=[hbm] * 8,
        out_specs=vmem,
        scratch_shapes=[
            pltpu.SMEM(decay_rate.shape, F32),
            pltpu.SMEM(doc_lengths.shape, jnp.int32),
            pltpu.VMEM((rows, features), BF16),
            pltpu.VMEM((rows, features), BF16),
            pltpu.VMEM((rows, features), BF16),
            pltpu.VMEM(carry_state.shape, F32),
            pltpu.VMEM((1, features), F32),
            pltpu.VMEM(order.shape, jnp.int32),
            dma((8,)),
            pltpu.VMEM((rows, features), F32),
            pltpu.VMEM((half, width, width), F32),
            pltpu.VMEM((half, width + 16, width), jnp.int16),
            pltpu.VMEM((half, width + 16, width), jnp.int16),
            pltpu.VMEM((half, width + 16, width), jnp.int16),
            pltpu.VMEM((reach, half, width + 16, width), jnp.int16),
            pltpu.VMEM((half, width, width), F32),
            pltpu.VMEM((half, width + 16, width), jnp.int16),
            pltpu.VMEM((half, width + 16, width), jnp.int16),
            pltpu.VMEM((8, rows), F32),
            pltpu.VMEM((n_head - 1, 8, rows), F32),
            dma((half,)), dma((half,)),
            dma((reach, half)), dma((reach, half)), dma((half,)),
            dma((half,)), dma((half,)),
            dma((n_head - 1,)), dma((n_head - 1,)),
        ],
        compiler_params=pltpu.CompilerParams(
            collective_id=0, has_side_effects=True, vmem_limit_bytes=64 * 1024 * 1024
        ),
    )(decay_rate, doc_lengths, queries, key_rows, value_rows, carry_state, norm_gain.reshape(1, features), order)


def solution(mesh):
    return jax.shard_map(
        shards,
        mesh=mesh,
        in_specs=(
            P("ctx", "head"),
            P("ctx", "head"),
            P("ctx", "head"),
            P("head", None, None),
            P("head"),
            P("head"),
            P("ctx", None),
            P(),
        ),
        out_specs=P("ctx", "head"),
        check_vma=False,
    )
```

```python
import functools

import jax
import jax.numpy as jnp
from jax import lax
from jax.experimental import pallas as pl
from jax.experimental.pallas import tpu as pltpu
from jax.sharding import PartitionSpec as P

F32 = jnp.float32
BF16 = jnp.bfloat16
MESH = pl.DeviceIdType.MESH


def split(x):
    high = x.astype(BF16)
    return high, (x - high.astype(F32)).astype(BF16)


def dot(a, b, contract):
    return lax.dot_general(a, b, ((contract[:1], contract[1:]), ((), ())), preferred_element_type=F32)


def two_term(a, b, contract):
    width = b.shape[1]
    both = dot(a, jnp.concatenate(split(b), axis=1), contract)
    return both[:, :width] + both[:, width:]


def coded(x):
    top = jnp.maximum(jnp.max(jnp.abs(x), axis=0, keepdims=True), 1e-30)
    level = jnp.ceil(jnp.log2(top) * 16.0)
    counts = jnp.round(x * (jnp.exp2(level * -0.0625) * 32760.0))
    rows = jnp.concatenate([counts, jnp.broadcast_to(level, (16, x.shape[1]))], axis=0)
    return rows.astype(jnp.int32).astype(jnp.int16)


def decoded(ref, index):
    whole = ref[index].astype(jnp.int32).astype(F32)
    width = whole.shape[1]
    return whole[:width] * (jnp.exp2(whole[width : width + 1] * 0.0625) * (1.0 / 32760.0))


def kernel(
    n_ctx, n_head, reach,
    rate_hbm, docs_hbm, q_hbm, k_hbm, v_hbm, carry_hbm, gain_hbm, order_hbm, out_hbm,
    rate_ref, docs_ref, q_ref, k_ref, v_ref, carry_ref, gain_ref, order_ref, load_sem, out_ref, store_sem,
    attn, pair, pair_in, away, layer, landed, entering, onward, arrived, squares, squares_in,
    pair_send, pair_recv, layer_send, layer_recv, wrap_send, onward_send, onward_recv, sq_send, sq_recv,
):
    rows, features = q_ref.shape
    heads = rate_ref.shape[0]
    width = features // heads
    half = heads // 2
    n_docs = docs_ref.shape[0]
    spill = rows // 4
    keep = rows - spill
    tokens = n_ctx * rows
    n_pairs = n_ctx // 2
    d = lax.axis_index("ctx")
    g = lax.axis_index("head")
    u = d // 2
    y = lax.rem(d, 2)
    partner = d + 1 - 2 * y
    mine = y * half
    other = (1 - y) * half

    inner = u + 1 < n_pairs

    def forwards(b):
        return inner & (u >= b - 1)

    def wraps(b):
        return u == n_pairs - b

    def receives(b):
        return (u >= b) | (u == 0)

    loads = {}
    operands = (
        (order_hbm, order_ref), (docs_hbm, docs_ref), (rate_hbm, rate_ref), (v_hbm, v_ref),
        (k_hbm, k_ref), (q_hbm, q_ref), (carry_hbm, carry_ref), (gain_hbm, gain_ref),
    )
    for n, (source, held) in enumerate(operands):
        loads[id(held)] = pltpu.make_async_copy(source, held, load_sem.at[n])
        if n < 5:
            loads[id(held)].start()

    barrier = pltpu.get_barrier_semaphore()
    pl.semaphore_signal(barrier, inc=1, device_id=(partner, g), device_id_type=MESH)
    for j in range(1, n_head):
        pl.semaphore_signal(
            barrier, inc=1, device_id=(d, lax.rem(g + n_head - j, n_head)), device_id_type=MESH
        )

    @pl.when(u > 0)
    def _():
        pl.semaphore_signal(barrier, inc=1, device_id=(d - 2, g), device_id_type=MESH)
    expected = n_head + inner.astype(jnp.int32)
    for b in range(1, reach + 1):
        @pl.when(u == 0)
        def _():
            pl.semaphore_signal(barrier, inc=1, device_id=(2 * (n_pairs - b) + y, g), device_id_type=MESH)
        expected = expected + wraps(b).astype(jnp.int32)

    for held in (q_ref, carry_ref, gain_ref):
        loads[id(held)].start()
    for held in (order_ref, docs_ref, rate_ref):
        loads[id(held)].wait()

    base = jnp.where(d == 0, tokens, d * rows) - spill
    last = d * rows + keep - 1
    chosen = (order_ref[...] == lax.broadcasted_iota(jnp.int32, (rows, rows), 0)).astype(F32).astype(BF16)
    index = lax.broadcasted_iota(jnp.int32, (rows, rows), 0).astype(F32).astype(BF16)
    along = lax.broadcasted_iota(jnp.int32, (16, rows), 1).astype(F32).astype(BF16)

    def position(slot):
        kept_at = (d * rows).astype(F32)
        moved_at = (base - keep).astype(F32)
        return slot + jnp.where(slot < keep, kept_at, moved_at)

    down = position(dot(chosen, index, (1, 0)))
    across = position(dot(along, chosen, (1, 1)))[0:1]
    pos = down[:, :width]

    pair_last = 2 * u * rows + rows + keep - 1
    first_last = 2 * u * rows + keep - 1
    pair_base = jnp.where(u == 0, tokens, 2 * u * rows) - spill
    marks = (last, pair_last, first_last, pair_base - 1)

    def over_documents(step, state):
        if n_docs <= 32:
            for n in range(n_docs):
                state = step(n, state)
            return state
        return lax.fori_loop(0, n_docs, step, state)

    def scalar_starts(n, carried):
        edge, starts = carried
        edge = edge + docs_ref[n]
        return edge, tuple(jnp.where(m >= edge, edge, s) for m, s in zip(marks, starts))

    def row_starts(n, carried):
        edge, begin = carried
        edge = edge + docs_ref[n]
        mark = edge.astype(F32)
        return edge, jnp.where(pos >= mark, mark, begin)

    zero = jnp.int32(0)
    last_begin, pair_begin, first_begin, base_begin = over_documents(scalar_starts, (zero, (zero,) * 4))[1]

    inf = jnp.float32(jnp.inf)

    def decay(h, steps):
        return jnp.exp(-rate_ref[h] * steps)

    def factor(h, steps, holds):
        return decay(h, jnp.full((1, width), jnp.where(holds, jnp.float32(steps), inf)))

    def columns(ref, h):
        return ref[:, pl.ds(pl.multiple_of(h * width, width), width)]

    to_last = jnp.where((pos <= last.astype(F32)) & (pos >= last_begin.astype(F32)), last.astype(F32) - pos, inf)

    def own_state(h):
        weighted = columns(v_ref, h).astype(F32) * decay(h, to_last)
        return two_term(columns(k_ref, h), weighted, (0, 0))

    def copy(src, dst, send, recv, target):
        return pltpu.make_async_remote_copy(
            src_ref=src, dst_ref=dst, send_sem=send, recv_sem=recv, device_id=target, device_id_type=MESH
        )

    loads[id(v_ref)].wait()
    loads[id(k_ref)].wait()

    pair_copies = []
    for i in range(half):
        away[i] = coded(own_state(other + i))
        if i == 0:
            pl.semaphore_wait(barrier, expected)
        c = copy(away.at[i], pair_in.at[i], pair_send.at[i], pair_recv.at[i], (partner, g))
        c.start()
        pair_copies.append(c)
    for i in range(half):
        pair[i] = own_state(mine + i)

    begin = over_documents(row_starts, (zero, jnp.zeros((rows, width), F32)))[1]
    gap = down - across
    begins = jnp.concatenate([begin] * (rows // width), axis=1)
    gap = jnp.where((gap >= 0) & (across >= begins), gap, inf)
    to_carry = jnp.where(begin == 0, pos + 1, inf)
    to_base = jnp.where(
        (pos >= base.astype(F32)) & (begin < base.astype(F32)), pos - (base - 1).astype(F32), inf
    )

    def add_local(h):
        cols = slice(h * width, (h + 1) * width)
        q, v = q_ref[:, cols], v_ref[:, cols]
        weights = dot(q, k_ref[:, cols], (1, 1)) * decay(h, gap)
        high, low = split(weights)
        local = dot(high, v, (1, 0)) + dot(low, v, (1, 0))
        attn[:, cols] = local + two_term(q, carry_ref[h], (1, 0)) * decay(h, to_carry)

    loads[id(q_ref)].wait()
    loads[id(carry_ref)].wait()

    def forward_copy(b, i):
        source = layer.at[i] if b == 1 else landed.at[b - 2, i]
        target = lax.rem(d + 2, n_ctx)
        return copy(source, landed.at[b - 1, i], layer_send.at[b - 1, i], layer_recv.at[b - 1, i], (target, g))

    def wrap_copy(b, i):
        return copy(layer.at[i], landed.at[b - 1, i], wrap_send.at[i], layer_recv.at[b - 1, i], (y, g))

    def forward(b, i):
        @pl.when(u >= b - 1)
        def _():
            forward_copy(b - 1, i).wait_recv()

        @pl.when(forwards(b))
        def _():
            forward_copy(b, i).start()

    is_first = y == 0
    for i in range(half):
        pair_copies[i].wait_recv()
        theirs, ours = decoded(pair_in, i), pair[i]
        first = jnp.where(is_first, ours, theirs)
        second = jnp.where(is_first, theirs, ours)
        layer[i] = coded(second + factor(mine + i, rows, pair_begin <= pair_last - rows) * first)
        pair[i] = first
        @pl.when(forwards(1))
        def _():
            forward_copy(1, i).start()
        for b in range(1, reach + 1):
            @pl.when(wraps(b))
            def _():
                wrap_copy(b, i).start()
    hops = [(b, i) for b in range(2, reach + 1) for i in range(half)]
    for h in range(heads):
        add_local(h)
        if h >= 1 and hops:
            forward(*hops.pop(0))
    for hop in hops:
        forward(*hop)

    def add_incoming(h, incoming):
        total = columns(attn, h) + two_term(columns(q_ref, h), incoming, (1, 0)) * decay(h, to_base)
        attn[:, pl.ds(pl.multiple_of(h * width, width), width)] = total
        return total * total

    onward_copies = []
    kept = []
    for i in range(half):
        h = mine + i
        entering[i] = jnp.zeros((width, width), F32)
        for b in range(1, reach + 1):
            @pl.when(receives(b))
            def _():
                @pl.when((u == 0) | (b == reach))
                def _():
                    forward_copy(b, i).wait_recv()

                steps = 2 * rows * (b - 1)
                fade = factor(h, steps, base_begin <= pair_base - 1 - steps)
                entering[i] += fade * decoded(landed, (b - 1, i))
        before_first = entering[i]
        before_second = pair[i] + factor(h, rows, first_begin <= first_last - rows) * before_first
        onward[i] = coded(jnp.where(is_first, before_second, before_first))
        c = copy(onward.at[i], arrived.at[i], onward_send.at[i], onward_recv.at[i], (partner, g))
        c.start()
        onward_copies.append(c)
        kept.append(jnp.where(is_first, before_first, before_second))
    power = jnp.zeros((rows, width), F32)
    for i in range(half):
        power += add_incoming(mine + i, kept[i])
    for i in range(half):
        onward_copies[i].wait_recv()
        power += add_incoming(other + i, decoded(arrived, i))

    ones = jnp.ones((16, width), BF16)
    high, low = split(power)
    squares[...] = (dot(ones, high, (1, 1)) + dot(ones, low, (1, 1)))[:8]
    sq_copies = []
    for j in range(1, n_head):
        c = copy(
            squares, squares_in.at[j - 1], sq_send.at[j - 1], sq_recv.at[j - 1], (d, lax.rem(g + j, n_head))
        )
        c.start()
        sq_copies.append(c)
    total = squares[...]
    for j in range(1, n_head):
        sq_copies[j - 1].wait_recv()
        total = total + squares_in[j - 1]
    scale = lax.rsqrt(total / jnp.float32(features * n_head) + 1e-5)
    scale = jnp.broadcast_to(scale[0:1], (width, rows)).T
    loads[id(gain_ref)].wait()

    def store(h):
        cols = slice(h * width, (h + 1) * width)
        return pltpu.make_async_copy(out_ref.at[:, cols], out_hbm.at[:, cols], store_sem.at[h])

    for h in range(heads):
        cols = slice(h * width, (h + 1) * width)
        out_ref[:, cols] = (attn[:, cols] * scale * gain_ref[:, cols]).astype(BF16)
        store(h).start()

    for h in range(heads):
        store(h).wait()
    for c in pair_copies + onward_copies + sq_copies:
        c.wait_send()
    for i in range(half):
        for b in range(1, reach + 1):
            @pl.when(forwards(b))
            def _():
                forward_copy(b, i).wait_send()

            @pl.when(wraps(b))
            def _():
                wrap_copy(b, i).wait_send()


def hand_over(parts, source, out, sem):
    size = source.shape[0] // parts
    copies = [
        pltpu.make_async_copy(source.at[pl.ds(n * size, size)], out.at[pl.ds(n * size, size)], sem.at[n])
        for n in range(parts)
    ]
    for c in copies:
        c.start()
    for c in copies:
        c.wait()


def shards(queries, key_rows, value_rows, carry_state, decay_rate, norm_gain, order, doc_lengths):
    rows, features = queries.shape
    heads, width, _ = carry_state.shape
    n_ctx, n_head = lax.axis_size("ctx"), lax.axis_size("head")
    longest = min(n_ctx * rows // 2, 2048)
    reach = -(-longest // (2 * rows))
    half = heads // 2
    hbm = pl.BlockSpec(memory_space=pltpu.HBM)
    dma = pltpu.SemaphoreType.DMA
    result = pl.pallas_call(
        functools.partial(kernel, n_ctx, n_head, reach),
        out_shape=jax.ShapeDtypeStruct((rows, features), BF16),
        in_specs=[hbm] * 8,
        out_specs=hbm,
        scratch_shapes=[
            pltpu.SMEM(decay_rate.shape, F32),
            pltpu.SMEM(doc_lengths.shape, jnp.int32),
            pltpu.VMEM((rows, features), BF16),
            pltpu.VMEM((rows, features), BF16),
            pltpu.VMEM((rows, features), BF16),
            pltpu.VMEM(carry_state.shape, F32),
            pltpu.VMEM((1, features), F32),
            pltpu.VMEM(order.shape, jnp.int32),
            dma((8,)),
            pltpu.VMEM((rows, features), BF16),
            dma((heads,)),
            pltpu.VMEM((rows, features), F32),
            pltpu.VMEM((half, width, width), F32),
            pltpu.VMEM((half, width + 16, width), jnp.int16),
            pltpu.VMEM((half, width + 16, width), jnp.int16),
            pltpu.VMEM((half, width + 16, width), jnp.int16),
            pltpu.VMEM((reach, half, width + 16, width), jnp.int16),
            pltpu.VMEM((half, width, width), F32),
            pltpu.VMEM((half, width + 16, width), jnp.int16),
            pltpu.VMEM((half, width + 16, width), jnp.int16),
            pltpu.VMEM((8, rows), F32),
            pltpu.VMEM((n_head - 1, 8, rows), F32),
            dma((half,)), dma((half,)),
            dma((reach, half)), dma((reach, half)), dma((half,)),
            dma((half,)), dma((half,)),
            dma((n_head - 1,)), dma((n_head - 1,)),
        ],
        compiler_params=pltpu.CompilerParams(
            collective_id=0, has_side_effects=True, vmem_limit_bytes=64 * 1024 * 1024
        ),
    )(decay_rate, doc_lengths, queries, key_rows, value_rows, carry_state, norm_gain.reshape(1, features), order)
    parts = 8
    return pl.pallas_call(
        functools.partial(hand_over, parts),
        out_shape=jax.ShapeDtypeStruct((rows, features), BF16),
        in_specs=[hbm],
        out_specs=hbm,
        scratch_shapes=[dma((parts,))],
        compiler_params=pltpu.CompilerParams(vmem_limit_bytes=64 * 1024 * 1024),
    )(result)


def solution(mesh):
    return jax.shard_map(
        shards,
        mesh=mesh,
        in_specs=(
            P("ctx", "head"),
            P("ctx", "head"),
            P("ctx", "head"),
            P("head", None, None),
            P("head"),
            P("head"),
            P("ctx", None),
            P(),
        ),
        out_specs=P("ctx", "head"),
        check_vma=False,
    )
```

```python
import functools

import jax
import jax.numpy as jnp
from jax import lax
from jax.experimental import pallas as pl
from jax.experimental.pallas import tpu as pltpu
from jax.sharding import PartitionSpec as P

F32 = jnp.float32
BF16 = jnp.bfloat16
MESH = pl.DeviceIdType.MESH


def split(x):
    high = x.astype(BF16)
    return high, (x - high.astype(F32)).astype(BF16)


def dot(a, b, contract):
    return lax.dot_general(a, b, ((contract[:1], contract[1:]), ((), ())), preferred_element_type=F32)


def two_term(a, b, contract):
    width = b.shape[1]
    both = dot(a, jnp.concatenate(split(b), axis=1), contract)
    return both[:, :width] + both[:, width:]


def coded(x):
    top = jnp.maximum(jnp.max(jnp.abs(x), axis=0, keepdims=True), 1e-30)
    level = jnp.ceil(jnp.log2(top) * 16.0)
    counts = jnp.round(x * (jnp.exp2(level * -0.0625) * 32760.0))
    rows = jnp.concatenate([counts, jnp.broadcast_to(level, (16, x.shape[1]))], axis=0)
    return rows.astype(jnp.int32).astype(jnp.int16)


def decoded(ref, index):
    whole = ref[index].astype(jnp.int32).astype(F32)
    width = whole.shape[1]
    return whole[:width] * (jnp.exp2(whole[width : width + 1] * 0.0625) * (1.0 / 32760.0))


def kernel(
    n_ctx, n_head, reach,
    rate_hbm, docs_hbm, q_hbm, k_hbm, v_hbm, carry_hbm, order_hbm, out_ref,
    rate_ref, docs_ref, q_ref, k_ref, v_ref, carry_ref, order_ref, load_sem,
    attn, pair, pair_in, away, layer, landed, entering, onward, arrived, squares, squares_in,
    pair_send, pair_recv, layer_send, layer_recv, wrap_send, onward_send, onward_recv, sq_send, sq_recv,
):
    rows, features = q_ref.shape
    heads = rate_ref.shape[0]
    width = features // heads
    half = heads // 2
    n_docs = docs_ref.shape[0]
    spill = rows // 4
    keep = rows - spill
    tokens = n_ctx * rows
    n_pairs = n_ctx // 2
    d = lax.axis_index("ctx")
    g = lax.axis_index("head")
    u = d // 2
    y = lax.rem(d, 2)
    partner = d + 1 - 2 * y
    mine = y * half
    other = (1 - y) * half

    inner = u + 1 < n_pairs

    def forwards(b):
        return inner & (u >= b - 1)

    def wraps(b):
        return u == n_pairs - b

    def receives(b):
        return (u >= b) | (u == 0)

    loads = {}
    operands = (
        (order_hbm, order_ref), (docs_hbm, docs_ref), (rate_hbm, rate_ref), (v_hbm, v_ref),
        (k_hbm, k_ref), (q_hbm, q_ref), (carry_hbm, carry_ref),
    )
    for n, (source, held) in enumerate(operands):
        loads[id(held)] = pltpu.make_async_copy(source, held, load_sem.at[n])
        loads[id(held)].start()

    barrier = pltpu.get_barrier_semaphore()
    pl.semaphore_signal(barrier, inc=1, device_id=(partner, g), device_id_type=MESH)
    for j in range(1, n_head):
        pl.semaphore_signal(
            barrier, inc=1, device_id=(d, lax.rem(g + n_head - j, n_head)), device_id_type=MESH
        )

    @pl.when(u > 0)
    def _():
        pl.semaphore_signal(barrier, inc=1, device_id=(d - 2, g), device_id_type=MESH)
    expected = n_head + inner.astype(jnp.int32)
    for b in range(1, reach + 1):
        @pl.when(u == 0)
        def _():
            pl.semaphore_signal(barrier, inc=1, device_id=(2 * (n_pairs - b) + y, g), device_id_type=MESH)
        expected = expected + wraps(b).astype(jnp.int32)

    for held in (order_ref, docs_ref, rate_ref):
        loads[id(held)].wait()

    base = jnp.where(d == 0, tokens, d * rows) - spill
    last = d * rows + keep - 1
    chosen = (order_ref[...] == lax.broadcasted_iota(jnp.int32, (rows, rows), 0)).astype(F32).astype(BF16)
    index = lax.broadcasted_iota(jnp.int32, (rows, rows), 0).astype(F32).astype(BF16)
    along = lax.broadcasted_iota(jnp.int32, (16, rows), 1).astype(F32).astype(BF16)

    def position(slot):
        kept_at = (d * rows).astype(F32)
        moved_at = (base - keep).astype(F32)
        return slot + jnp.where(slot < keep, kept_at, moved_at)

    down = position(dot(chosen, index, (1, 0)))
    across = position(dot(along, chosen, (1, 1)))[0:1]
    pos = down[:, :width]

    pair_last = 2 * u * rows + rows + keep - 1
    first_last = 2 * u * rows + keep - 1
    pair_base = jnp.where(u == 0, tokens, 2 * u * rows) - spill
    marks = (last, pair_last, first_last, pair_base - 1)

    def over_documents(step, state):
        if n_docs <= 32:
            for n in range(n_docs):
                state = step(n, state)
            return state
        return lax.fori_loop(0, n_docs, step, state)

    def scalar_starts(n, carried):
        edge, starts = carried
        edge = edge + docs_ref[n]
        return edge, tuple(jnp.where(m >= edge, edge, s) for m, s in zip(marks, starts))

    def row_starts(n, carried):
        edge, begin = carried
        edge = edge + docs_ref[n]
        mark = edge.astype(F32)
        return edge, jnp.where(pos >= mark, mark, begin)

    zero = jnp.int32(0)
    last_begin, pair_begin, first_begin, base_begin = over_documents(scalar_starts, (zero, (zero,) * 4))[1]

    inf = jnp.float32(jnp.inf)

    def decay(h, steps):
        return jnp.exp(-rate_ref[h] * steps)

    def factor(h, steps, holds):
        return decay(h, jnp.full((1, width), jnp.where(holds, jnp.float32(steps), inf)))

    def columns(ref, h):
        return ref[:, pl.ds(pl.multiple_of(h * width, width), width)]

    to_last = jnp.where((pos <= last.astype(F32)) & (pos >= last_begin.astype(F32)), last.astype(F32) - pos, inf)

    def own_state(h):
        weighted = columns(v_ref, h).astype(F32) * decay(h, to_last)
        return two_term(columns(k_ref, h), weighted, (0, 0))

    def copy(src, dst, send, recv, target):
        return pltpu.make_async_remote_copy(
            src_ref=src, dst_ref=dst, send_sem=send, recv_sem=recv, device_id=target, device_id_type=MESH
        )

    loads[id(v_ref)].wait()
    loads[id(k_ref)].wait()

    pair_copies = []
    for i in range(half):
        away[i] = coded(own_state(other + i))
        if i == 0:
            pl.semaphore_wait(barrier, expected)
        c = copy(away.at[i], pair_in.at[i], pair_send.at[i], pair_recv.at[i], (partner, g))
        c.start()
        pair_copies.append(c)
    for i in range(half):
        pair[i] = own_state(mine + i)

    begin = over_documents(row_starts, (zero, jnp.zeros((rows, width), F32)))[1]
    gap = down - across
    begins = jnp.concatenate([begin] * (rows // width), axis=1)
    gap = jnp.where((gap >= 0) & (across >= begins), gap, inf)
    to_carry = jnp.where(begin == 0, pos + 1, inf)
    to_base = jnp.where(
        (pos >= base.astype(F32)) & (begin < base.astype(F32)), pos - (base - 1).astype(F32), inf
    )

    def add_local(h):
        cols = slice(h * width, (h + 1) * width)
        q, v = q_ref[:, cols], v_ref[:, cols]
        weights = dot(q, k_ref[:, cols], (1, 1)) * decay(h, gap)
        high, low = split(weights)
        local = dot(high, v, (1, 0)) + dot(low, v, (1, 0))
        attn[:, cols] = local + two_term(q, carry_ref[h], (1, 0)) * decay(h, to_carry)

    loads[id(q_ref)].wait()
    loads[id(carry_ref)].wait()

    def forward_copy(b, i):
        source = layer.at[i] if b == 1 else landed.at[b - 2, i]
        target = lax.rem(d + 2, n_ctx)
        return copy(source, landed.at[b - 1, i], layer_send.at[b - 1, i], layer_recv.at[b - 1, i], (target, g))

    def wrap_copy(b, i):
        return copy(layer.at[i], landed.at[b - 1, i], wrap_send.at[i], layer_recv.at[b - 1, i], (y, g))

    def forward(b, i):
        @pl.when(u >= b - 1)
        def _():
            forward_copy(b - 1, i).wait_recv()

        @pl.when(forwards(b))
        def _():
            forward_copy(b, i).start()

    is_first = y == 0
    for i in range(half):
        pair_copies[i].wait_recv()
        theirs, ours = decoded(pair_in, i), pair[i]
        first = jnp.where(is_first, ours, theirs)
        second = jnp.where(is_first, theirs, ours)
        layer[i] = coded(second + factor(mine + i, rows, pair_begin <= pair_last - rows) * first)
        pair[i] = first
        @pl.when(forwards(1))
        def _():
            forward_copy(1, i).start()
        for b in range(1, reach + 1):
            @pl.when(wraps(b))
            def _():
                wrap_copy(b, i).start()
    hops = [(b, i) for b in range(2, reach + 1) for i in range(half)]
    for h in range(heads):
        add_local(h)
        if h >= 1 and hops:
            forward(*hops.pop(0))
    for hop in hops:
        forward(*hop)

    def add_incoming(h, incoming):
        total = columns(attn, h) + two_term(columns(q_ref, h), incoming, (1, 0)) * decay(h, to_base)
        attn[:, pl.ds(pl.multiple_of(h * width, width), width)] = total
        return total * total

    onward_copies = []
    kept = []
    for i in range(half):
        h = mine + i
        entering[i] = jnp.zeros((width, width), F32)
        for b in range(1, reach + 1):
            @pl.when(receives(b))
            def _():
                @pl.when((u == 0) | (b == reach))
                def _():
                    forward_copy(b, i).wait_recv()

                steps = 2 * rows * (b - 1)
                fade = factor(h, steps, base_begin <= pair_base - 1 - steps)
                entering[i] += fade * decoded(landed, (b - 1, i))
        before_first = entering[i]
        before_second = pair[i] + factor(h, rows, first_begin <= first_last - rows) * before_first
        onward[i] = coded(jnp.where(is_first, before_second, before_first))
        c = copy(onward.at[i], arrived.at[i], onward_send.at[i], onward_recv.at[i], (partner, g))
        c.start()
        onward_copies.append(c)
        kept.append(jnp.where(is_first, before_first, before_second))
    power = jnp.zeros((rows, width), F32)
    for i in range(half):
        power += add_incoming(mine + i, kept[i])
    for i in range(half):
        onward_copies[i].wait_recv()
        power += add_incoming(other + i, decoded(arrived, i))

    ones = jnp.ones((16, width), BF16)
    high, low = split(power)
    squares[...] = (dot(ones, high, (1, 1)) + dot(ones, low, (1, 1)))[:8]
    sq_copies = []
    for j in range(1, n_head):
        c = copy(
            squares, squares_in.at[j - 1], sq_send.at[j - 1], sq_recv.at[j - 1], (d, lax.rem(g + j, n_head))
        )
        c.start()
        sq_copies.append(c)
    total = squares[...]
    for j in range(1, n_head):
        sq_copies[j - 1].wait_recv()
        total = total + squares_in[j - 1]
    scale = lax.rsqrt(total / jnp.float32(features * n_head) + 1e-5)
    scale = jnp.broadcast_to(scale[0:1], (width, rows)).T
    for h in range(heads):
        cols = slice(h * width, (h + 1) * width)
        out_ref[:, cols] = attn[:, cols] * scale

    for c in pair_copies + onward_copies + sq_copies:
        c.wait_send()
    for i in range(half):
        for b in range(1, reach + 1):
            @pl.when(forwards(b))
            def _():
                forward_copy(b, i).wait_send()

            @pl.when(wraps(b))
            def _():
                wrap_copy(b, i).wait_send()


def shards(queries, key_rows, value_rows, carry_state, decay_rate, norm_gain, order, doc_lengths):
    rows, features = queries.shape
    heads, width, _ = carry_state.shape
    n_ctx, n_head = lax.axis_size("ctx"), lax.axis_size("head")
    longest = min(n_ctx * rows // 2, 2048)
    reach = -(-longest // (2 * rows))
    half = heads // 2
    vmem = pl.BlockSpec(memory_space=pltpu.VMEM)
    hbm = pl.BlockSpec(memory_space=pltpu.HBM)
    dma = pltpu.SemaphoreType.DMA
    scaled = pl.pallas_call(
        functools.partial(kernel, n_ctx, n_head, reach),
        out_shape=jax.ShapeDtypeStruct((rows, features), F32),
        in_specs=[hbm] * 7,
        out_specs=vmem,
        scratch_shapes=[
            pltpu.SMEM(decay_rate.shape, F32),
            pltpu.SMEM(doc_lengths.shape, jnp.int32),
            pltpu.VMEM((rows, features), BF16),
            pltpu.VMEM((rows, features), BF16),
            pltpu.VMEM((rows, features), BF16),
            pltpu.VMEM(carry_state.shape, F32),
            pltpu.VMEM(order.shape, jnp.int32),
            dma((7,)),
            pltpu.VMEM((rows, features), F32),
            pltpu.VMEM((half, width, width), F32),
            pltpu.VMEM((half, width + 16, width), jnp.int16),
            pltpu.VMEM((half, width + 16, width), jnp.int16),
            pltpu.VMEM((half, width + 16, width), jnp.int16),
            pltpu.VMEM((reach, half, width + 16, width), jnp.int16),
            pltpu.VMEM((half, width, width), F32),
            pltpu.VMEM((half, width + 16, width), jnp.int16),
            pltpu.VMEM((half, width + 16, width), jnp.int16),
            pltpu.VMEM((8, rows), F32),
            pltpu.VMEM((n_head - 1, 8, rows), F32),
            dma((half,)), dma((half,)),
            dma((reach, half)), dma((reach, half)), dma((half,)),
            dma((half,)), dma((half,)),
            dma((n_head - 1,)), dma((n_head - 1,)),
        ],
        compiler_params=pltpu.CompilerParams(
            collective_id=0, has_side_effects=True, vmem_limit_bytes=64 * 1024 * 1024
        ),
    )(decay_rate, doc_lengths, queries, key_rows, value_rows, carry_state, order)
    return (scaled * norm_gain[None, :]).astype(BF16)


def solution(mesh):
    return jax.shard_map(
        shards,
        mesh=mesh,
        in_specs=(
            P("ctx", "head"),
            P("ctx", "head"),
            P("ctx", "head"),
            P("head", None, None),
            P("head"),
            P("head"),
            P("ctx", None),
            P(),
        ),
        out_specs=P("ctx", "head"),
        check_vma=False,
    )
```
